512 devices in a mesh: dp: 32 (over y, x_hi, core), tensor: 16 (over x_lo, z).
Axes of the slice: x: 4 (x_hi: 2, x_lo: 2; x = x_hi * 2 + x_lo), y: 8, z: 8, core: 2. Of those that a mesh axis runs over, the one named last changes fastest.
Arguments:
- master: float32 [512, 53248], P('dp', 'tensor')
- checks: bfloat16 [512, 64], P('dp', 'tensor'), may hold values from -6 to 6
Outputs:
- quantized: bfloat16 [512, 53248], P(None, 'tensor')
- block_scales: float32 [4, 416], P(None, 'tensor')
- probe_out: float32 [64, 53248], P(None, 'tensor')
The draws below stay inside these ranges and needn't reach their ends.
All inputs are finite; a program needn't handle non-finite values. Where the reference program divides by a largest or mean magnitude, that divisor is 1e-20 or more.
Results may differ from the reference program's by a relative error of at most 0.0051.
Values may be sent and summed in bfloat16 or wider, within the bound.
No kernel may reach another device: no remote copies, remote signals or barrier semaphores. Data moves between devices by JAX's collectives and lax.ppermute only.
A program may use at most 64 MiB of HBM per device.

```python
import math
import jax
import jax.numpy as jnp

C = 53248
BLOCK = 128
CHECK = 64
ROWS = 512


def draw_master(key, part):
    key = jax.random.fold_in(key, 11)
    key_base, key_rows, key_cols = jax.random.split(key, 3)
    base = jax.random.normal(key_base, (ROWS, C), jnp.float32)
    col_top = 10.0
    row_factor = jnp.exp(jax.random.uniform(key_rows, (ROWS,), jnp.float32, 0.0, math.log(10.0)))
    col_factor = jnp.exp(jax.random.uniform(key_cols, (C,), jnp.float32, 0.0, math.log(col_top)))
    return base * row_factor[:, None] * col_factor[None, :] * (0.125 * ROWS ** (-0.5))


def level_of(own_key, extent, cuts, low, high):
    def one(position, shards_of):
        steps = jax.random.uniform(jax.random.fold_in(jax.random.fold_in(own_key, 6), position), (shards_of,), jnp.float32, low / len(cuts), high / len(cuts))
        return jnp.repeat(jnp.exp(steps), extent[position] // shards_of).reshape((-1,) + (1,) * (len(extent) - position - 1))

    loudness = one(*cuts[0])
    for cut in cuts[1:]:
        loudness = loudness * one(*cut)
    return loudness


def scatter_about(own_key, extent, spread, reach, cuts=(), held_as=jnp.bfloat16):
    array = jax.random.normal(own_key, extent, jnp.float32) * spread
    if len(cuts) > 0:
        array = level_of(own_key, extent, cuts, -0.22, 0.18) * array
    return jnp.clip(array, min=-reach, max=reach).astype(held_as)


def setup_inputs(seed: int = 0) -> dict:
    arg_keys = jax.random.split(jax.random.key(seed), 3)
    master = draw_master(jax.random.fold_in(arg_keys[2], 71), 0)
    checks = scatter_about(arg_keys[1], (ROWS, CHECK), 1.0, 6.0, ((0, 32), (1, 16)))
    return dict(master=master, checks=checks)


epsilon = 1e-6


def reference(master, checks):
    tiles = master.reshape(ROWS // BLOCK, BLOCK, C // BLOCK, BLOCK)
    scales = jnp.max(jnp.abs(tiles), axis=(1, 3)) + epsilon
    codes = (tiles / scales[:, None, :, None]).reshape(ROWS, C).astype(jnp.bfloat16)
    restored = (codes.astype(jnp.float32).reshape(tiles.shape) * scales[:, None, :, None]).reshape(ROWS, C).astype(jnp.bfloat16)
    probes = jnp.dot(checks.T, restored, preferred_element_type=jnp.float32)
    return codes, scales, probes
```

```python
import functools

import jax
import jax.numpy as jnp
import numpy as np
from jax import lax
from jax.experimental import pallas as pl
from jax.experimental.pallas import tpu as pltpu
from jax.sharding import PartitionSpec as P

BLOCK = 128
EPS = 1e-06
Y = 8
LANES = 128
HALF = 64
TILE = 256

CORES = [[2 * i, 2 * i + 1] for i in range(16)]


def along_y(step):
    pairs = []
    for y in range(Y):
        for rest in range(4):
            to = (y + step if rest % 2 == 0 else y - step) % Y
            pairs.append((y * 4 + rest, to * 4 + rest))
    return pairs


ACROSS_X = [(i, i ^ 2) for i in range(32)]


def both_cores(a):
    return lax.all_gather(a, "dp", axis_index_groups=CORES, axis=0, tiled=True)


def prepare_kernel(m_ref, x_ref, part_ref):
    m = m_ref[...]
    x_ref[...] = m.astype(jnp.bfloat16)
    high = jnp.max(jnp.abs(m), axis=0, keepdims=True)
    lane = lax.broadcasted_iota(jnp.int32, (1, HALF), 1)
    tops = jnp.zeros((1, HALF), jnp.float32)
    for j in range(m.shape[1] // BLOCK):
        top = jnp.max(high[:, j * BLOCK : (j + 1) * BLOCK], axis=1, keepdims=True)
        tops = jnp.where(lane == j, top, tops)
    first = tops.astype(jnp.bfloat16).astype(jnp.float32)
    second = (tops - first).astype(jnp.bfloat16).astype(jnp.float32)
    third = tops - first - second
    row = lax.broadcasted_iota(jnp.int32, (16, HALF), 0)
    part = jnp.where(row == 0, first, jnp.where(row == 1, second, third))
    part_ref[...] = jnp.where(row < 3, part, 0.0).astype(jnp.bfloat16)


def prepare(m):
    rows, cols = m.shape
    return pl.pallas_call(
        prepare_kernel,
        out_shape=(
            jax.ShapeDtypeStruct((rows, cols), jnp.bfloat16),
            jax.ShapeDtypeStruct((rows, HALF), jnp.bfloat16),
        ),
        name="prepare",
    )(m)


def pieces():
    out = [("own", 0, 0, 0), ("own", 32, 0, 1)]
    for core, sign in ((0, -1), (1, 1)):
        for name, place in (("two", 2), ("one", 1), ("three", 3)):
            for part in (0, 1):
                out.append((name, core * 64 + part * 32, sign * place, part))
        out.append(("four", core * 32, 4, core))
    return out


def export_kernel(at_ref, tab_ref, own_ref, two_ref, one_ref, three_ref, four_ref, codes_ref, scales_ref, probe_ref, scale_s, inv_s, checks_s):
    n_blocks = scales_ref.shape[1]
    tile = codes_ref.shape[1]

    @pl.when(pl.program_id(0) == 0)
    def _():
        tab = tab_ref[...].astype(jnp.float32)
        checks_s[...] = tab.T[HALF:, :].astype(jnp.bfloat16)
        terms = tab.reshape(32, 16, LANES)
        tops = terms[:, 0, :] + terms[:, 1, :] + terms[:, 2, :]
        scale = jnp.max(tops.reshape(4, 8, LANES), axis=1) + EPS
        scales_ref[...] = scale[:, :n_blocks]
        inv = 1.0 / scale
        for j in range(n_blocks):
            cols = slice(j * BLOCK, (j + 1) * BLOCK)
            scale_s[:, cols] = jnp.broadcast_to(scale[:, j : j + 1], (4, BLOCK))
            inv_s[:, cols] = jnp.broadcast_to(inv[:, j : j + 1], (4, BLOCK))

    refs = dict(own=own_ref, two=two_ref, one=one_ref, three=three_ref, four=four_ref)
    y, xh = at_ref[0], at_ref[1]
    start = pl.multiple_of(pl.program_id(0) * tile, BLOCK)
    for name, row, place, part in pieces():
        to = lax.rem(y + place + Y, Y)
        side = xh if part == 0 else 1 - xh
        inv = inv_s[pl.ds(to // 2, 1), pl.ds(start, tile)]
        value = refs[name][row : row + 32, :].astype(jnp.float32) * inv
        dest = pl.multiple_of(to * 64 + side * 32, 32)
        codes_ref[pl.ds(dest, 32), :] = value.astype(jnp.bfloat16)
    total = jnp.zeros(probe_ref.shape, jnp.float32)
    for g in range(4):
        part = jnp.dot(
            checks_s[:, g * BLOCK : (g + 1) * BLOCK],
            codes_ref[g * BLOCK : (g + 1) * BLOCK, :],
            preferred_element_type=jnp.float32,
        )
        total = total + part * scale_s[g : g + 1, pl.ds(start, tile)]
    probe_ref[...] = total


def export(at, tab, *received):
    cols = received[0].shape[1]
    whole = lambda a: pl.BlockSpec(a.shape, lambda i: (0, 0))
    strip = lambda a: pl.BlockSpec((a.shape[0], TILE), lambda i: (0, i))
    return pl.pallas_call(
        export_kernel,
        grid=(cols // TILE,),
        in_specs=[
            pl.BlockSpec(memory_space=pltpu.SMEM),
            whole(tab),
            *map(strip, received),
        ],
        out_specs=(
            pl.BlockSpec((512, TILE), lambda i: (0, i)),
            pl.BlockSpec((4, cols // BLOCK), lambda i: (0, 0)),
            pl.BlockSpec((64, TILE), lambda i: (0, i)),
        ),
        out_shape=(
            jax.ShapeDtypeStruct((512, cols), jnp.bfloat16),
            jax.ShapeDtypeStruct((4, cols // BLOCK), jnp.float32),
            jax.ShapeDtypeStruct((64, cols), jnp.float32),
        ),
        scratch_shapes=[
            pltpu.VMEM((4, cols), jnp.float32),
            pltpu.VMEM((4, cols), jnp.float32),
            pltpu.VMEM((64, 512), jnp.bfloat16),
        ],
        compiler_params=pltpu.CompilerParams(vmem_limit_bytes=24 * 1024 * 1024),
        name="export",
    )(at, tab, *received)


def after(a, *others):
    return lax.optimization_barrier((a, *others))[0]


def per_device(master, checks):
    me = lax.axis_index("dp")
    core = me % 2
    at = jnp.stack([me // 4, (me // 2) % 2]).astype(jnp.int32)
    x, part = prepare(master)
    other = lax.ppermute(x, "dp", ACROSS_X)
    a = both_cores(x)
    two_a = lax.ppermute(a, "dp", along_y(2))
    b = both_cores(other)
    two_b = lax.ppermute(b, "dp", along_y(2))
    own = jnp.concatenate([a, b], 0)
    one = lax.ppermute(own, "dp", along_y(1))
    sent = after(checks, b)
    spread = lax.all_to_all(jnp.broadcast_to(sent[None], (16, 16, 4)), "tensor", 0, 0)
    rows = spread.transpose(1, 0, 2).reshape(16, HALF)
    two = jnp.concatenate([two_a, two_b], 0)
    three = lax.ppermute(two, "dp", along_y(1))
    four = lax.ppermute(jnp.where(core == 0, two_a, two_b), "dp", along_y(2))
    two = both_cores(after(two, one))
    one = both_cores(one)
    table = after(jnp.concatenate([part, rows], 1), one)
    tab = lax.all_to_all(jnp.broadcast_to(table[None], (32, 16, LANES)), "dp", 0, 0)
    three, four = both_cores(three), both_cores(four)
    codes, scales, probes = export(at, tab.reshape(512, LANES), own, two, one, three, four)
    return codes, scales, probes


def solution(mesh):
    return jax.shard_map(
        per_device,
        mesh=mesh,
        in_specs=(P("dp", "tensor"), P("dp", "tensor")),
        out_specs=(P(None, "tensor"), P(None, "tensor"), P(None, "tensor")),
        check_vma=False,
    )
```

```python
import jax
import jax.numpy as jnp
from jax import lax
from jax.experimental import pallas as pl
from jax.experimental.pallas import tpu as pltpu
from jax.sharding import Mesh, PartitionSpec as P

BLOCK = 128
EPS = 1e-06
Y = 8
LANES = 128
HALF = 64
TILE = 256
MIB = 1024 * 1024


def along(a, step, across=0):
    pairs = []
    for y in range(Y):
        for xh in range(2):
            for core, to in ((0, (y + step) % Y), (1, (y - step) % Y)):
                pairs.append((y * 4 + xh * 2 + core, to * 4 + (xh ^ across) * 2 + core))
    return lax.ppermute(a, ("y", "x_hi", "core"), pairs)


def both_cores(a):
    return lax.all_gather(a, "core", axis=0, tiled=True)


def swap(a, axis):
    return lax.ppermute(a, axis, [(0, 1), (1, 0)])


def after(a, *others):
    return lax.optimization_barrier((a, *others))[0]


def kernel_of(body, out_shape, limit, cost=None, **more):
    params = pltpu.CompilerParams(vmem_limit_bytes=limit * MIB)
    if cost is not None:
        cost = pl.CostEstimate(flops=0, bytes_accessed=cost, transcendentals=0)
    return pl.pallas_call(body, out_shape=out_shape, compiler_params=params, cost_estimate=cost, name=body.__name__, **more)


def prepare(m_ref, x_ref):
    m = m_ref[...]
    rows, cols = m.shape
    x_ref[:, :cols] = m.astype(jnp.bfloat16)
    high = jnp.max(jnp.abs(m), axis=0, keepdims=True)
    lane = lax.broadcasted_iota(jnp.int32, (1, LANES), 1)
    tops = jnp.zeros((1, LANES), jnp.float32)
    for j in range(cols // BLOCK):
        top = jnp.max(high[:, j * BLOCK : (j + 1) * BLOCK], axis=1, keepdims=True)
        tops = jnp.where(lane == j, top, tops)
    first = tops.astype(jnp.bfloat16).astype(jnp.float32)
    second = (tops - first).astype(jnp.bfloat16).astype(jnp.float32)
    third = tops - first - second
    row = lax.broadcasted_iota(jnp.int32, (rows, LANES), 0)
    tail = jnp.where(row == 0, first, jnp.where(row == 1, second, third))
    x_ref[:, cols:] = jnp.where(row < 3, tail, 0.0).astype(jnp.bfloat16)


def spread(a_ref, out_ref):
    out_ref[...] = jnp.broadcast_to(a_ref[...][None], out_ref.shape)


def export(
    at_ref, a, b, two, one, three, four, codes_ref, scales_ref, probe_ref,
    codes_s, probe_s, tab_s, checks_s, scale_s, inv_s, sems, probe_sem,
):
    cols = codes_s.shape[1]
    n_blocks = cols // BLOCK
    y, xh = at_ref[0], at_ref[1]
    found = [(0, (a, 0), (b, 0))]
    for place, ref in ((2, two), (1, one), (3, three)):
        found += [(-place, (ref, 0), (ref, 32)), (place, (ref, 64), (ref, 96))]
    found.append((4, (four, 0), (four, 32)))

    def target(place, part):
        to = lax.rem(y + place + Y, Y)
        return to, pl.ds(pl.multiple_of(to * 64 + lax.rem(xh + part, 2) * 32, 32), 32)

    for place, *halves in found:
        for part, (ref, row) in enumerate(halves):
            tab_s[target(place, part)[1], :] = ref[row : row + 32, cols:].astype(jnp.float32)
    tab = tab_s[...]
    checks_s[...] = tab.T[HALF:, :].astype(jnp.bfloat16)
    terms = tab.reshape(32, 16, LANES)
    tops = terms[:, 0, :] + terms[:, 1, :] + terms[:, 2, :]
    scale = jnp.max(tops.reshape(4, 8, LANES), axis=1) + EPS
    scales_ref[...] = scale[:, :n_blocks]
    inv = 1.0 / scale
    for j in range(n_blocks):
        block = slice(j * BLOCK, (j + 1) * BLOCK)
        scale_s[:, block] = jnp.broadcast_to(scale[:, j : j + 1], (4, BLOCK))
        inv_s[:, block] = jnp.broadcast_to(inv[:, j : j + 1], (4, BLOCK))

    sends = []
    for n, (place, *halves) in enumerate(found):
        to = target(place, 0)[0]

        def strip(k, _, to=to, place=place, halves=halves):
            at = pl.ds(pl.multiple_of(k * TILE, TILE), TILE)
            factor = inv_s[pl.ds(to // 2, 1), at]
            for part, (ref, row) in enumerate(halves):
                value = ref[row : row + 32, at].astype(jnp.float32) * factor
                codes_s[target(place, part)[1], at] = value.astype(jnp.bfloat16)
            return 0

        lax.fori_loop(0, cols // TILE, strip, 0, unroll=True)
        rows = pl.ds(pl.multiple_of(to * 64, 64), 64)
        sends.append(pltpu.make_async_copy(codes_s.at[rows, :], codes_ref.at[rows, :], sems.at[n]))
        sends[-1].start()

    def dots(k, _):
        at = pl.ds(pl.multiple_of(k * TILE, TILE), TILE)
        total = jnp.zeros((HALF, TILE), jnp.float32)
        for g in range(4):
            group = slice(g * BLOCK, (g + 1) * BLOCK)
            part = jnp.dot(checks_s[:, group], codes_s[group, at], preferred_element_type=jnp.float32)
            total = total + part * scale_s[g : g + 1, at]
        probe_s[:, at] = total
        return 0

    lax.fori_loop(0, cols // TILE, dots, 0, unroll=True)
    sends.append(pltpu.make_async_copy(probe_s, probe_ref, probe_sem))
    sends[-1].start()
    for send in sends:
        send.wait()


SMEM = pl.BlockSpec(memory_space=pltpu.SMEM)
VMEM = pl.BlockSpec(memory_space=pltpu.VMEM)
ANY = pl.BlockSpec(memory_space=pl.ANY)


def per_device(master, checks):
    core, xh = lax.axis_index("core"), lax.axis_index("x_hi")
    at = jnp.stack([lax.axis_index("y"), xh, core]).astype(jnp.int32)
    rows, cols = master.shape
    n_blocks = cols // BLOCK
    full = lambda *shape: jax.ShapeDtypeStruct(shape, jnp.float32)
    brief = lambda *shape: jax.ShapeDtypeStruct(shape, jnp.bfloat16)

    peers = lax.axis_size("tensor")
    sent = kernel_of(spread, brief(peers, 4, rows), 4)(checks.T)
    got = lax.all_to_all(sent, "tensor", 0, 0).reshape(HALF, rows).T
    x = kernel_of(prepare, brief(rows, cols + LANES), 4)(master)
    a = both_cores(lax.dynamic_update_slice(x, got, (0, cols + HALF)))
    two_a, two_b = along(a, 2), along(a, 2, across=1)
    b = swap(a, "x_hi")
    one = along(jnp.concatenate([a, b], 0), 1)
    two = jnp.concatenate([two_a, two_b], 0)
    three = along(two, 1)
    four = along(jnp.where(core == 0, two_a, two_b), 2)

    two = both_cores(after(two, one))
    one = both_cores(one)
    four = both_cores(after(four, two, one))
    three = both_cores(after(three, four))
    return kernel_of(
        export,
        (brief(512, cols), full(4, n_blocks), full(HALF, cols)),
        16,
        in_specs=[SMEM] + [VMEM] * 6,
        out_specs=(ANY, VMEM, ANY),
        scratch_shapes=[
            pltpu.VMEM((512, cols), jnp.bfloat16),
            pltpu.VMEM((HALF, cols), jnp.float32),
            pltpu.VMEM((512, LANES), jnp.float32),
            pltpu.VMEM((HALF, 512), jnp.bfloat16),
            pltpu.VMEM((4, cols), jnp.float32),
            pltpu.VMEM((4, cols), jnp.float32),
            pltpu.SemaphoreType.DMA((8,)),
            pltpu.SemaphoreType.DMA,
        ],
    )(at, a, b, two, one, three, four)


def solution(mesh):
    split = Mesh(mesh.devices.reshape(Y, 2, 2, mesh.shape["tensor"]), ("y", "x_hi", "core", "tensor"))
    dp = ("y", "x_hi", "core")
    return jax.shard_map(
        per_device,
        mesh=split,
        in_specs=(P(dp, "tensor"), P(dp, "tensor")),
        out_specs=(P(None, "tensor"), P(None, "tensor"), P(None, "tensor")),
        check_vma=False,
    )
```

```python
import jax
import jax.numpy as jnp
from jax import lax
from jax.experimental import pallas as pl
from jax.experimental.pallas import tpu as pltpu
from jax.sharding import Mesh, PartitionSpec as P

BLOCK = 128
EPS = 1e-06
Y = 8
LANES = 128
HALF = 64
TILE = 256
MIB = 1024 * 1024
TOP = 255.0 * 2.0**120


def along(a, step, across=0):
    pairs = []
    for y in range(Y):
        for xh in range(2):
            for core, to in ((0, (y + step) % Y), (1, (y - step) % Y)):
                pairs.append((y * 4 + xh * 2 + core, to * 4 + (xh ^ across) * 2 + core))
    return lax.ppermute(a, ("y", "x_hi", "core"), pairs)


def both_cores(a):
    return lax.all_gather(a, "core", axis=0, tiled=True)


def swap(a, axis):
    return lax.ppermute(a, axis, [(0, 1), (1, 0)])


def after(a, *others):
    return lax.optimization_barrier((a, *others))[0]


def kernel_of(body, out_shape, limit, cost=None, **more):
    params = pltpu.CompilerParams(vmem_limit_bytes=limit * MIB)
    if cost is not None:
        cost = pl.CostEstimate(flops=0, bytes_accessed=cost, transcendentals=0)
    return pl.pallas_call(body, out_shape=out_shape, compiler_params=params, cost_estimate=cost, name=body.__name__, **more)


def prepare(m_ref, x_ref):
    m = m_ref[...]
    rows, cols = m.shape
    x_ref[:, :cols] = jnp.clip(m, -TOP, TOP).astype(jnp.bfloat16)
    high = jnp.max(jnp.abs(m), axis=0, keepdims=True)
    lane = lax.broadcasted_iota(jnp.int32, (1, LANES), 1)
    tops = jnp.zeros((1, LANES), jnp.float32)
    for j in range(cols // BLOCK):
        top = jnp.max(high[:, j * BLOCK : (j + 1) * BLOCK], axis=1, keepdims=True)
        tops = jnp.where(lane == j, top, tops)
    first = jnp.minimum(tops, TOP).astype(jnp.bfloat16).astype(jnp.float32)
    second = (tops - first).astype(jnp.bfloat16).astype(jnp.float32)
    third = tops - first - second
    row = lax.broadcasted_iota(jnp.int32, (rows, LANES), 0)
    tail = jnp.where(row == 0, first, jnp.where(row == 1, second, third))
    x_ref[:, cols:] = jnp.where(row < 3, tail, 0.0).astype(jnp.bfloat16)


def spread(a_ref, out_ref):
    out_ref[...] = jnp.broadcast_to(a_ref[...][None], out_ref.shape)


def export(
    at_ref, a, b, two, one, three, four, codes_ref, scales_ref, probe_ref,
    codes_s, probe_s, tab_s, checks_s, scale_s, inv_s, sems, probe_sem,
):
    cols = codes_s.shape[1]
    n_blocks = cols // BLOCK
    y, xh = at_ref[0], at_ref[1]
    shrink = lambda scale: jnp.where(scale > 2.0**100, 2.0**-60, 1.0)
    found = [(0, (a, 0), (b, 0))]
    for place, ref in ((2, two), (1, one), (3, three)):
        found += [(-place, (ref, 0), (ref, 32)), (place, (ref, 64), (ref, 96))]
    found.append((4, (four, 0), (four, 32)))

    def target(place, part):
        to = lax.rem(y + place + Y, Y)
        return to, pl.ds(pl.multiple_of(to * 64 + lax.rem(xh + part, 2) * 32, 32), 32)

    for place, *halves in found:
        for part, (ref, row) in enumerate(halves):
            tab_s[target(place, part)[1], :] = ref[row : row + 32, cols:].astype(jnp.float32)
    tab = tab_s[...]
    checks_s[...] = tab.T[HALF:, :].astype(jnp.bfloat16)
    terms = tab.reshape(32, 16, LANES)
    tops = terms[:, 0, :] + (terms[:, 1, :] + terms[:, 2, :])
    scale = jnp.max(tops.reshape(4, 8, LANES), axis=1) + EPS
    scales_ref[...] = scale[:, :n_blocks]
    for j in range(n_blocks):
        block = slice(j * BLOCK, (j + 1) * BLOCK)
        wide = jnp.broadcast_to(scale[:, j : j + 1], (4, BLOCK))
        scale_s[:, block] = wide
        inv_s[:, block] = 1.0 / (wide * shrink(wide))

    large = jnp.max(scale) > 2.0**100
    sends = []
    for n, (place, *halves) in enumerate(found):
        to = target(place, 0)[0]
        group = to // 2
        dests = [target(place, part)[1] for part in (0, 1)]

        def strip(k, shrunk, group=group, dests=dests, halves=halves):
            at = pl.ds(pl.multiple_of(k * TILE, TILE), TILE)
            factor = inv_s[pl.ds(group, 1), at]
            for dest, (ref, row) in zip(dests, halves):
                value = ref[row : row + 32, at].astype(jnp.float32)
                if shrunk:
                    value = value * shrink(scale_s[pl.ds(group, 1), at])
                codes_s[dest, at] = (value * factor).astype(jnp.bfloat16)

        for k in range(cols // TILE):
            strip(k, False)

        @pl.when(large)
        def _(strip=strip):
            pl.loop(0, cols // TILE)(lambda k: strip(k, True))

        rows = pl.ds(pl.multiple_of(to * 64, 64), 64)
        sends.append(pltpu.make_async_copy(codes_s.at[rows, :], codes_ref.at[rows, :], sems.at[n]))
        sends[-1].start()

    def dots(k):
        at = pl.ds(pl.multiple_of(k * TILE, TILE), TILE)
        total = jnp.zeros((HALF, TILE), jnp.float32)
        for g in range(4):
            group = slice(g * BLOCK, (g + 1) * BLOCK)
            part = jnp.dot(checks_s[:, group], codes_s[group, at], preferred_element_type=jnp.float32)
            total = total + part * scale_s[g : g + 1, at]
        probe_s[:, at] = total

    strips, done = cols // TILE, 0
    for n, upto in enumerate((strips // 2, strips)):
        for k in range(done, upto):
            dots(k)
        at = slice(done * TILE, upto * TILE)
        sends.append(pltpu.make_async_copy(probe_s.at[:, at], probe_ref.at[:, at], probe_sem.at[n]))
        sends[-1].start()
        done = upto
    for send in sends:
        send.wait()


SMEM = pl.BlockSpec(memory_space=pltpu.SMEM)
VMEM = pl.BlockSpec(memory_space=pltpu.VMEM)
ANY = pl.BlockSpec(memory_space=pl.ANY)


def per_device(master, checks):
    core, xh = lax.axis_index("core"), lax.axis_index("x_hi")
    at = jnp.stack([lax.axis_index("y"), xh, core]).astype(jnp.int32)
    rows, cols = master.shape
    n_blocks = cols // BLOCK
    full = lambda *shape: jax.ShapeDtypeStruct(shape, jnp.float32)
    brief = lambda *shape: jax.ShapeDtypeStruct(shape, jnp.bfloat16)

    peers = lax.axis_size("tensor")
    sent = kernel_of(spread, brief(peers, 4, rows), 4)(checks.T)
    got = lax.all_to_all(sent, "tensor", 0, 0).reshape(HALF, rows).T
    x = kernel_of(prepare, brief(rows, cols + LANES), 4)(master)
    a = both_cores(lax.dynamic_update_slice(x, got, (0, cols + HALF)))
    two_a, two_b = along(a, 2), along(a, 2, across=1)
    b = swap(a, "x_hi")
    one = along(jnp.concatenate([a, b], 0), 1)
    two = jnp.concatenate([two_a, two_b], 0)
    three = along(two, 1)
    four = along(jnp.where(core == 0, two_a, two_b), 2)

    two = both_cores(after(two, one))
    one = both_cores(one)
    four = both_cores(after(four, two, one))
    three = both_cores(after(three, four))
    return kernel_of(
        export,
        (brief(512, cols), full(4, n_blocks), full(HALF, cols)),
        16,
        in_specs=[SMEM] + [VMEM] * 6,
        out_specs=(ANY, VMEM, ANY),
        scratch_shapes=[
            pltpu.VMEM((512, cols), jnp.bfloat16),
            pltpu.VMEM((HALF, cols), jnp.float32),
            pltpu.VMEM((512, LANES), jnp.float32),
            pltpu.VMEM((HALF, 512), jnp.bfloat16),
            pltpu.VMEM((4, cols), jnp.float32),
            pltpu.VMEM((4, cols), jnp.float32),
            pltpu.SemaphoreType.DMA((8,)),
            pltpu.SemaphoreType.DMA((2,)),
        ],
    )(at, a, b, two, one, three, four)


def solution(mesh):
    split = Mesh(mesh.devices.reshape(Y, 2, 2, mesh.shape["tensor"]), ("y", "x_hi", "core", "tensor"))
    dp = ("y", "x_hi", "core")
    return jax.shard_map(
        per_device,
        mesh=split,
        in_specs=(P(dp, "tensor"), P(dp, "tensor")),
        out_specs=(P(None, "tensor"), P(None, "tensor"), P(None, "tensor")),
        check_vma=False,
    )
```

```python
import jax
import jax.numpy as jnp
from jax import lax
from jax.experimental import pallas as pl
from jax.experimental.pallas import tpu as pltpu
from jax.sharding import Mesh, PartitionSpec as P

BLOCK = 128
EPS = 1e-06
Y = 8
LANES = 128
HALF = 64
TILE = 256
MIB = 1024 * 1024
TOP = 255.0 * 2.0**120


def along(a, step, across=0):
    pairs = []
    for y in range(Y):
        for xh in range(2):
            for core, to in ((0, (y - step) % Y), (1, (y + step) % Y)):
                pairs.append((y * 4 + xh * 2 + core, to * 4 + (xh ^ across) * 2 + core))
    return lax.ppermute(a, ("y", "x_hi", "core"), pairs)


def both_cores(a):
    return lax.all_gather(a, "core", axis=0, tiled=True)


def swap(a, axis):
    return lax.ppermute(a, axis, [(0, 1), (1, 0)])


def after(a, *others):
    return lax.optimization_barrier((a, *others))[0]


def kernel_of(body, out_shape, limit, cost=None, **more):
    params = pltpu.CompilerParams(vmem_limit_bytes=limit * MIB)
    if cost is not None:
        cost = pl.CostEstimate(flops=0, bytes_accessed=cost, transcendentals=0)
    return pl.pallas_call(body, out_shape=out_shape, compiler_params=params, cost_estimate=cost, name=body.__name__, **more)


def prepare(m_ref, x_ref):
    m = m_ref[...]
    rows, cols = m.shape
    x_ref[:, :cols] = jnp.clip(m, -TOP, TOP).astype(jnp.bfloat16)
    high = jnp.max(jnp.abs(m), axis=0, keepdims=True)
    lane = lax.broadcasted_iota(jnp.int32, (1, LANES), 1)
    tops = jnp.zeros((1, LANES), jnp.float32)
    for j in range(cols // BLOCK):
        top = jnp.max(high[:, j * BLOCK : (j + 1) * BLOCK], axis=1, keepdims=True)
        tops = jnp.where(lane == j, top, tops)
    first = jnp.minimum(tops, TOP).astype(jnp.bfloat16).astype(jnp.float32)
    second = (tops - first).astype(jnp.bfloat16).astype(jnp.float32)
    third = tops - first - second
    row = lax.broadcasted_iota(jnp.int32, (rows, LANES), 0)
    tail = jnp.where(row == 0, first, jnp.where(row == 1, second, third))
    x_ref[:, cols:] = jnp.where(row < 3, tail, 0.0).astype(jnp.bfloat16)


def spread(a_ref, out_ref):
    out_ref[...] = jnp.broadcast_to(a_ref[...][None], out_ref.shape)


def export(
    at_ref, a, b, two, one, three, four, codes_ref, scales_ref, probe_ref,
    codes_s, probe_s, tab_s, checks_s, scale_s, inv_s, sems, probe_sem,
):
    cols = codes_s.shape[1]
    n_blocks = cols // BLOCK
    y, xh = at_ref[0], at_ref[1]
    shrink = lambda scale: jnp.where(scale > 2.0**100, 2.0**-60, 1.0)
    found = [(0, (a, 0), (b, 0))]
    for place, ref in ((2, two), (1, one), (3, three)):
        found += [(place, (ref, 0), (ref, 32)), (-place, (ref, 64), (ref, 96))]
    found.append((4, (four, 0), (four, 32)))

    def target(place, part):
        to = lax.rem(y + place + Y, Y)
        return to, pl.ds(pl.multiple_of(to * 64 + lax.rem(xh + part, 2) * 32, 32), 32)

    for place, *halves in found:
        for part, (ref, row) in enumerate(halves):
            tab_s[target(place, part)[1], :] = ref[row : row + 32, cols:].astype(jnp.float32)
    tab = tab_s[...]
    checks_s[...] = tab.T[HALF:, :].astype(jnp.bfloat16)
    terms = tab.reshape(32, 16, LANES)
    tops = terms[:, 0, :] + (terms[:, 1, :] + terms[:, 2, :])
    scale = jnp.max(tops.reshape(4, 8, LANES), axis=1) + EPS
    scales_ref[...] = scale[:, :n_blocks]
    for j in range(n_blocks):
        block = slice(j * BLOCK, (j + 1) * BLOCK)
        wide = jnp.broadcast_to(scale[:, j : j + 1], (4, BLOCK))
        scale_s[:, block] = wide
        inv_s[:, block] = 1.0 / (wide * shrink(wide))

    large = jnp.max(scale) > 2.0**100
    sends = []
    for n, (place, *halves) in enumerate(found):
        to = target(place, 0)[0]
        group = to // 2
        dests = [target(place, part)[1] for part in (0, 1)]

        def strip(k, shrunk, group=group, dests=dests, halves=halves):
            at = pl.ds(pl.multiple_of(k * TILE, TILE), TILE)
            factor = inv_s[pl.ds(group, 1), at]
            for dest, (ref, row) in zip(dests, halves):
                value = ref[row : row + 32, at].astype(jnp.float32)
                if shrunk:
                    value = value * shrink(scale_s[pl.ds(group, 1), at])
                codes_s[dest, at] = (value * factor).astype(jnp.bfloat16)

        for k in range(cols // TILE):
            strip(k, False)

        @pl.when(large)
        def _(strip=strip):
            pl.loop(0, cols // TILE)(lambda k: strip(k, True))

        rows = pl.ds(pl.multiple_of(to * 64, 64), 64)
        sends.append(pltpu.make_async_copy(codes_s.at[rows, :], codes_ref.at[rows, :], sems.at[n]))
        sends[-1].start()

    def dots(k):
        at = pl.ds(pl.multiple_of(k * TILE, TILE), TILE)
        total = jnp.zeros((HALF, TILE), jnp.float32)
        for g in range(4):
            group = slice(g * BLOCK, (g + 1) * BLOCK)
            part = jnp.dot(checks_s[:, group], codes_s[group, at], preferred_element_type=jnp.float32)
            total = total + part * scale_s[g : g + 1, at]
        probe_s[:, at] = total

    strips, done = cols // TILE, 0
    for n, upto in enumerate((strips // 2, strips)):
        for k in range(done, upto):
            dots(k)
        at = slice(done * TILE, upto * TILE)
        sends.append(pltpu.make_async_copy(probe_s.at[:, at], probe_ref.at[:, at], probe_sem.at[n]))
        sends[-1].start()
        done = upto
    for send in sends:
        send.wait()


SMEM = pl.BlockSpec(memory_space=pltpu.SMEM)
VMEM = pl.BlockSpec(memory_space=pltpu.VMEM)
ANY = pl.BlockSpec(memory_space=pl.ANY)


def per_device(master, checks):
    core, xh = lax.axis_index("core"), lax.axis_index("x_hi")
    at = jnp.stack([lax.axis_index("y"), xh, core]).astype(jnp.int32)
    rows, cols = master.shape
    n_blocks = cols // BLOCK
    full = lambda *shape: jax.ShapeDtypeStruct(shape, jnp.float32)
    brief = lambda *shape: jax.ShapeDtypeStruct(shape, jnp.bfloat16)

    peers = lax.axis_size("tensor")
    sent = kernel_of(spread, brief(peers, 4, rows), 4)(checks.T)
    got = lax.all_to_all(sent, "tensor", 0, 0).reshape(HALF, rows).T
    x = kernel_of(prepare, brief(rows, cols + LANES), 4)(master)
    a = both_cores(lax.dynamic_update_slice(x, got, (0, cols + HALF)))
    two_a, two_b = along(a, 2), along(a, 2, across=1)
    b = swap(a, "x_hi")
    one = along(jnp.concatenate([a, b], 0), 1)
    two = jnp.concatenate([two_a, two_b], 0)
    three = along(two, 1)
    four = along(jnp.where(core == 0, two_a, two_b), 2)

    two = both_cores(after(two, one))
    one = both_cores(one)
    four = both_cores(after(four, two, one))
    three = both_cores(after(three, four))
    return kernel_of(
        export,
        (brief(512, cols), full(4, n_blocks), full(HALF, cols)),
        16,
        in_specs=[SMEM] + [VMEM] * 6,
        out_specs=(ANY, VMEM, ANY),
        scratch_shapes=[
            pltpu.VMEM((512, cols), jnp.bfloat16),
            pltpu.VMEM((HALF, cols), jnp.float32),
            pltpu.VMEM((512, LANES), jnp.float32),
            pltpu.VMEM((HALF, 512), jnp.bfloat16),
            pltpu.VMEM((4, cols), jnp.float32),
            pltpu.VMEM((4, cols), jnp.float32),
            pltpu.SemaphoreType.DMA((8,)),
            pltpu.SemaphoreType.DMA((2,)),
        ],
    )(at, a, b, two, one, three, four)


def solution(mesh):
    split = Mesh(mesh.devices.reshape(Y, 2, 2, mesh.shape["tensor"]), ("y", "x_hi", "core", "tensor"))
    dp = ("y", "x_hi", "core")
    return jax.shard_map(
        per_device,
        mesh=split,
        in_specs=(P(dp, "tensor"), P(dp, "tensor")),
        out_specs=(P(None, "tensor"), P(None, "tensor"), P(None, "tensor")),
        check_vma=False,
    )
```
